32 devices in a mesh: seq: 4 (over z), row: 2 (over core), col: 4 (over y, x).
Axes of the slice: x: 2, y: 2, z: 4, core: 2. Of those that a mesh axis runs over, the one named last changes fastest.
Arguments:
- tokens: bfloat16 [512, 4096], P('seq', 'row'), may hold values from -40 to 40
- block_order: int32 [8], replicated, may hold values from 0 to 7, as said below
- query_weight: bfloat16 [4096, 4096], P('row', 'col'), may hold values from -0.09375 to 0.09375
- key_weight: bfloat16 [4096, 1024], P('row', 'col'), may hold values from -0.09375 to 0.09375
- value_weight: bfloat16 [4096, 1024], P('row', 'col'), may hold values from -0.09375 to 0.09375
- output_weight: bfloat16 [4096, 4096], P('col'), may hold values from -0.09375 to 0.09375
Outputs:
- layer_out: float32 [512, 4096], P('seq', ('row', 'col'))
The draws below stay inside these ranges and needn't reach their ends.
Inputs may be any that keep to these rules, and one draw needn't show every extreme that they name: Slots 2 d and 2 d + 1 are the rows of device d along seq; for every d, block_order[2 d + 1] = 7 - block_order[2 d] with block_order[2 d] < 4, and every half-block appears once.
All inputs are finite; a program needn't handle non-finite values.
Results may differ from the reference program's by a relative error of at most 0.012.
The reference program's roundings to bfloat16 on the way (of `attended`) count: a program that leaves them out, or rounds other values in their place, can miss the bound.
Values may be sent and summed in bfloat16 or wider, within the bound.
A program may use at most 64 MiB of HBM per device.

```python
import jax
import jax.numpy as jnp
from jax import lax

D = 4096
H = 32
KV = 8
HD = 128
TOK_DEV = 128
TOKENS = 512
N_SEQ = 4


def draw_tokens(key, part):
    first_key = jax.random.fold_in(key, 0)
    base = jax.random.normal(first_key, (TOKENS, D), jnp.float32)
    values = base
    return jnp.clip(values, -40.0, 40.0).astype(jnp.bfloat16)


def draw_block_order(key, part):
    lower = jax.random.permutation(key, N_SEQ).astype(jnp.int32)
    upper = 2 * N_SEQ - 1 - lower
    return jnp.stack([lower, upper], axis=1).reshape(2 * N_SEQ).astype(jnp.int32)


def level_of(stream_key, shape, cuts, least, largest):
    level = 1.0
    for position, blocks in cuts:
        heights = jax.random.uniform(jax.random.fold_in(jax.random.fold_in(stream_key, 6), position), (blocks,), jnp.float32, least / len(cuts), largest / len(cuts))
        level = level * jnp.repeat(jnp.exp(heights), shape[position] // blocks).reshape((-1,) + (1,) * (len(shape) - 1 - position))
    return level


def noise(own_key, shape, deviation, reach, shards=(), held_as=jnp.bfloat16):
    result = jax.random.normal(own_key, shape, jnp.float32) * deviation
    if len(shards) > 0:
        result = level_of(own_key, shape, shards, -0.22, 0.18) * result
    return jnp.clip(result, min=-reach, max=reach).astype(held_as)


def setup_inputs(seed: int = 0) -> dict:
    key_of = jax.random.split(jax.random.key(seed), 7)
    return {
        "tokens": draw_tokens(jax.random.fold_in(key_of[6], 71), 0),
        "block_order": draw_block_order(jax.random.fold_in(key_of[6], 71), 0),
        "query_weight": noise(key_of[2], (D, H * HD), D ** -0.5, 0.09375, ((0, 2), (1, 4))),
        "key_weight": noise(key_of[3], (D, KV * HD), D ** -0.5, 0.09375, ((0, 2), (1, 4))),
        "value_weight": noise(key_of[4], (D, KV * HD), D ** -0.5, 0.09375, ((0, 2), (1, 4))),
        "output_weight": noise(key_of[5], (H * HD, D), (H * HD) ** -0.5, 0.09375, ((0, 4),)),
    }


rope_theta = 500000.0
large_negative = -1e30


def rotate(vectors, positions):
    half_width = vectors.shape[-1] // 2
    freqs = rope_theta ** (-(jnp.arange(half_width, dtype=jnp.float32) * 2.0 / vectors.shape[-1]))
    angles = positions.astype(jnp.float32)[:, None] * freqs[None, :]
    cosine = jnp.cos(angles)[:, None, :]
    sine = jnp.sin(angles)[:, None, :]
    first = vectors[..., :half_width]
    second = vectors[..., half_width:]
    return jnp.concatenate([first * cosine - second * sine, second * cosine + first * sine], axis=-1)


def token_positions(block_order, first_row, count, half_rows):
    rows_index = first_row + jnp.arange(count, dtype=jnp.int32)
    slots = rows_index // half_rows
    matched = slots[:, None] == jnp.arange(block_order.shape[0], dtype=jnp.int32)[None, :]
    chosen = jnp.sum(jnp.where(matched, block_order[None, :], 0), axis=1).astype(jnp.int32)
    return chosen * half_rows + rows_index % half_rows


def reference(tokens, block_order, query_weight, key_weight, value_weight, output_weight):
    total = tokens.shape[0]
    half_rows = TOK_DEV // 2
    positions = token_positions(block_order, 0, total, half_rows)
    queries = jnp.dot(tokens, query_weight, preferred_element_type=jnp.float32).reshape(total, H, HD)
    keys_all = jnp.dot(tokens, key_weight, preferred_element_type=jnp.float32).reshape(total, KV, HD)
    values_all = jnp.dot(tokens, value_weight, preferred_element_type=jnp.float32).reshape(total, KV, HD)
    queries = rotate(queries, positions).astype(jnp.bfloat16)
    keys_all = rotate(keys_all, positions).astype(jnp.bfloat16)
    values_all = values_all.astype(jnp.bfloat16)
    group_size = H // KV
    block_rows = min(total, 1024)
    blocks = total // block_rows
    grouped = queries.reshape(blocks, block_rows, KV, group_size, HD).transpose(2, 0, 1, 3, 4)
    query_pos = positions.reshape(blocks, block_rows)
    score_scale = HD ** -0.5

    def per_head(inputs):
        head_queries, head_keys, head_values = inputs
        keys_wide = head_keys.astype(jnp.float32)
        values_wide = head_values.astype(jnp.float32)

        def per_block(block_inputs):
            block_queries, block_pos = block_inputs
            scores = jnp.einsum("qhd,kd->qhk", block_queries.astype(jnp.float32), keys_wide) * score_scale
            visible = positions[None, None, :] <= block_pos[:, None, None]
            scores = jnp.where(visible, scores, large_negative)
            highest = jnp.max(scores, axis=-1, keepdims=True)
            weights = jnp.where(visible, jnp.exp(scores - highest), 0.0)
            denom = jnp.sum(weights, axis=-1)
            rounded = lax.optimization_barrier(weights.astype(jnp.bfloat16))
            mixed = jnp.einsum("qhk,kd->qhd", rounded.astype(jnp.float32), values_wide)
            return (mixed / denom[..., None]).astype(jnp.bfloat16)

        return lax.map(per_block, (head_queries, query_pos))

    attended = lax.map(per_head, (grouped, keys_all.transpose(1, 0, 2), values_all.transpose(1, 0, 2)))
    attended = attended.transpose(1, 2, 0, 3, 4).reshape(total, H * HD)
    return jnp.dot(attended, output_weight, preferred_element_type=jnp.float32)
```

```python
from functools import partial

import jax
import jax.numpy as jnp
import numpy as np
from jax import lax
from jax.experimental import pallas as pl
from jax.experimental.pallas import tpu as pltpu
from jax.sharding import PartitionSpec as P

H = 32
KV = 8
HD = 128
THETA = 500000.0
HIDDEN = -1e30
WIDE = 256
F32 = jnp.float32
BF16 = jnp.bfloat16


def rotary_table(half_rows, blocks):
    freqs = THETA ** (-2.0 * np.arange(HD // 2) / HD)
    starts = np.concatenate([np.arange(half_rows), half_rows * np.arange(blocks)])
    angles = starts[:, None] * freqs[None, :]
    cosine, sine = np.cos(angles), np.sin(angles)
    return np.concatenate([cosine, cosine, -sine, sine], axis=1).astype(np.float32)


def each(first, last, step):
    if last - first <= 8:
        for index in range(first, last):
            step(index)
    else:
        lax.fori_loop(first, last, lambda index, _: (step(index), 0)[1], 0)


def layer_kernel(
    seqs, cols,
    order_ref, x_hbm, wq_hbm, wk_hbm, wv_hbm, wo_hbm, table_hbm,
    out_ref,
    x, wkv, wq, wo, table, rot,
    kv_snd, kv_rcv, q_snd, q_rcv, q, kv, scores, att, att_peer, partial_own, rs_snd, rs_rcv,
    load_sem, wo_sem, core_send, core_recv, seq_send, seq_recv, col_send, col_recv,
):
    rows = x.shape[0]
    half = rows // 2
    heads = wq.shape[1] // 2 // HD
    width = heads * HD
    group = H // KV
    out_width = wo.shape[2]

    me_seq = lax.axis_index("seq")
    me_row = lax.axis_index("row")
    me_col = lax.axis_index("col")
    other = 1 - me_row

    def kv_columns(row):
        return pl.ds(pl.multiple_of(row * heads // group * HD, HD), HD)

    def q_columns(row):
        return pl.ds(pl.multiple_of(row * width, width), width)

    loads = [pltpu.make_async_copy(x_hbm, x, load_sem.at[0])]
    for slot, (source, row) in enumerate(
        [(wk_hbm, other), (wv_hbm, other), (wk_hbm, me_row), (wv_hbm, me_row)]
    ):
        loads.append(
            pltpu.make_async_copy(
                source.at[:, kv_columns(row)],
                wkv.at[:, pl.ds(slot * HD, HD)],
                load_sem.at[1 + slot],
            )
        )
    loads.append(pltpu.make_async_copy(table_hbm, table, load_sem.at[7]))
    for slot, row in enumerate([other, me_row]):
        loads.append(
            pltpu.make_async_copy(
                wq_hbm.at[:, q_columns(row)],
                wq.at[:, pl.ds(slot * width, width)],
                load_sem.at[5 + slot],
            )
        )
    for load in loads:
        load.start()
    load_x, load_kv, load_table, load_q = loads[0], loads[1:5], loads[5], loads[6:]

    def wo_load(step, part):
        target = lax.rem(me_col + step, cols)
        row = me_row if part == 0 else other
        first = pl.multiple_of((me_row * cols + target) * out_width, out_width)
        return pltpu.make_async_copy(
            wo_hbm.at[q_columns(row), pl.ds(first, out_width)],
            wo.at[step, pl.ds(part * width, width), :],
            wo_sem.at[step, part],
        )

    for part in range(2):
        for step in list(range(1, cols)) + [0]:
            wo_load(step, part).start()

    barrier = pltpu.get_barrier_semaphore()
    pl.semaphore_signal(barrier, inc=1, device_id={"row": other})
    each(1, seqs, lambda d: pl.semaphore_signal(
        barrier, inc=1, device_id={"seq": lax.rem(me_seq + d, seqs)}))
    each(1, cols, lambda d: pl.semaphore_signal(
        barrier, inc=1, device_id={"col": lax.rem(me_col + d, cols)}))

    load_table.wait()
    for part in range(2):
        cos_in = table[0:half, 0:HD]
        sin_in = table[0:half, HD:]
        start = table[pl.ds(half + order_ref[2 * me_seq + part], 1), :]
        cos_at, sin_at = start[:, :HD], start[:, HD:]
        here = pl.ds(part * half, half)
        rot[0, here, :] = cos_at * cos_in - sin_at * sin_in
        rot[1, here, :] = sin_at * cos_in + cos_at * sin_in

    def rotate(vectors):
        return vectors * rot[0] + pltpu.roll(vectors, HD // 2, 1) * rot[1]

    def to_core(source, target, index):
        return pltpu.make_async_remote_copy(
            src_ref=source, dst_ref=target,
            send_sem=core_send.at[index], recv_sem=core_recv.at[index],
            device_id={"row": other},
        )

    load_x.wait()
    load_kv[0].wait()
    load_kv[1].wait()
    kv_snd[...] = jnp.dot(x[...], wkv[:, : 2 * HD], preferred_element_type=F32).astype(kv_snd.dtype)
    pl.semaphore_wait(barrier, 1 + (seqs - 1) + (cols - 1))
    send_kv = to_core(kv_snd, kv_rcv, 0)
    send_kv.start()
    load_kv[2].wait()
    load_kv[3].wait()
    kv_own = jnp.dot(x[...], wkv[:, 2 * HD :], preferred_element_type=F32)
    send_kv.wait_recv()
    kv_sum = kv_own + kv_rcv[...].astype(F32)
    kv[me_seq, 0] = rotate(kv_sum[:, :HD]).astype(BF16)
    kv[me_seq, 1] = kv_sum[:, HD:].astype(BF16)

    def to_seq(d):
        return pltpu.make_async_remote_copy(
            src_ref=kv.at[me_seq], dst_ref=kv.at[me_seq],
            send_sem=seq_send.at[d], recv_sem=seq_recv.at[d],
            device_id={"seq": lax.rem(me_seq + d, seqs)},
        )

    def from_seq(d):
        source = lax.rem(me_seq - d + seqs, seqs)
        return pltpu.make_async_remote_copy(
            src_ref=kv.at[source], dst_ref=kv.at[source],
            send_sem=seq_send.at[d], recv_sem=seq_recv.at[d],
            device_id={"seq": lax.rem(me_seq + d, seqs)},
        )

    each(1, seqs, lambda d: to_seq(d).start())

    load_q[0].wait()
    for first in range(0, width, WIDE):
        q_snd[:, first : first + WIDE] = jnp.dot(
            x[...], wq[:, first : first + WIDE], preferred_element_type=F32
        ).astype(q_snd.dtype)
    send_q = to_core(q_snd, q_rcv, 1)
    send_q.start()
    load_q[1].wait()
    own = [
        jnp.dot(x[...], wq[:, width + first : width + first + WIDE], preferred_element_type=F32)
        for first in range(0, width, WIDE)
    ]
    send_q.wait_recv()
    for head in range(heads):
        at = head * HD
        summed = own[at // WIDE][:, at % WIDE : at % WIDE + HD] + q_rcv[:, at : at + HD].astype(F32)
        q[at : at + HD, :] = rotate(summed).astype(BF16)

    row_of = lax.broadcasted_iota(jnp.int32, (rows, 1), 0)
    lane_of = lax.broadcasted_iota(jnp.int32, (1, rows), 1)

    def positions(index, source):
        first, second = order_ref[2 * source] * half, order_ref[2 * source + 1] * half
        return jnp.where(index < half, first + index, second + (index - half))

    query_pos = positions(row_of, me_seq)

    def score(d):
        source = lax.rem(me_seq - d + seqs, seqs)
        visible = positions(lane_of, source) <= query_pos
        raw = lax.dot_general(
            q[...], kv[source, 0], (((1,), (1,)), ((), ())), preferred_element_type=F32
        )
        for head in range(heads):
            here = slice(head * rows, (head + 1) * rows)
            scores[source, here, :] = jnp.where(visible, raw[here], HIDDEN)

    score(0)

    def arrive(d):
        from_seq(d).wait_recv()
        score(d)

    each(1, seqs, arrive)

    stride = min(seqs, 4)
    best = scores[0]
    if seqs <= 8:
        for source in range(1, seqs):
            best = jnp.maximum(best, scores[source])
    else:
        best = lax.fori_loop(1, seqs, lambda s, b: jnp.maximum(b, scores[s]), best)
    top = jnp.max(best, axis=1, keepdims=True)
    factor = HD ** -0.5 * float(np.log2(np.e))

    def mix(index, carry):
        total, mixed = carry
        parts, values = [], []
        for inner in range(stride):
            source = index * stride + inner
            weights = jnp.exp2((scores[source] - top) * factor)
            total = total + weights
            parts.append(weights.astype(BF16))
            values.append(kv[source, 1])
        mixed = mixed + jnp.dot(
            jnp.concatenate(parts, axis=1), jnp.concatenate(values, axis=0),
            preferred_element_type=F32,
        )
        return total, mixed

    zero = jnp.zeros((heads * rows, HD), F32)
    if seqs <= 4:
        total, mixed = mix(0, (zero, zero))
    else:
        total, mixed = lax.fori_loop(0, seqs // stride, mix, (zero, zero))
    attended = (mixed / jnp.sum(total, axis=1, keepdims=True)).astype(BF16)
    for head in range(heads):
        att[:, head * HD : (head + 1) * HD] = attended[head * rows : (head + 1) * rows]
    send_att = to_core(att, att_peer, 2)
    send_att.start()

    steps = list(range(1, cols)) + [0]
    for step in steps:
        wo_load(step, 0).wait()
        partial_own[step] = jnp.dot(att[...], wo[step, :width, :], preferred_element_type=F32)
    send_att.wait_recv()

    def to_col(d):
        return pltpu.make_async_remote_copy(
            src_ref=rs_snd.at[d], dst_ref=rs_rcv.at[d],
            send_sem=col_send.at[d], recv_sem=col_recv.at[d],
            device_id={"col": lax.rem(me_col + d, cols)},
        )

    for step in steps:
        wo_load(step, 1).wait()
        summed = partial_own[step] + jnp.dot(
            att_peer[...], wo[step, width:, :], preferred_element_type=F32
        )
        if step == 0:
            partial_own[0] = summed
        else:
            rs_snd[step] = summed.astype(rs_snd.dtype)
            to_col(step).start()
    for d in range(1, cols):
        to_col(d).wait_recv()
    final = partial_own[0]
    for d in range(1, cols):
        final = final + rs_rcv[d].astype(F32)
    out_ref[...] = final

    send_kv.wait_send()
    send_q.wait_send()
    send_att.wait_send()
    each(1, seqs, lambda d: to_seq(d).wait_send())
    for d in range(1, cols):
        to_col(d).wait_send()


def body(seqs, cols, tokens, block_order, query_weight, key_weight, value_weight, output_weight):
    rows, depth = tokens.shape
    width = query_weight.shape[1] // 2
    out_width = output_weight.shape[1] // (2 * cols)
    heads = width // HD
    table = rotary_table(rows // 2, block_order.shape[0])
    anywhere = pl.BlockSpec(memory_space=pl.ANY)
    return pl.pallas_call(
        partial(layer_kernel, seqs, cols),
        out_shape=jax.ShapeDtypeStruct((rows, out_width), F32),
        in_specs=[pl.BlockSpec(memory_space=pltpu.SMEM)] + [anywhere] * 6,
        out_specs=pl.BlockSpec(memory_space=pltpu.VMEM),
        scratch_shapes=[
            pltpu.VMEM((rows, depth), BF16),
            pltpu.VMEM((depth, 4 * HD), BF16),
            pltpu.VMEM((depth, 2 * width), BF16),
            pltpu.VMEM((cols, 2 * width, out_width), BF16),
            pltpu.VMEM(table.shape, F32),
            pltpu.VMEM((2, rows, HD), F32),
            pltpu.VMEM((rows, 2 * HD), BF16),
            pltpu.VMEM((rows, 2 * HD), BF16),
            pltpu.VMEM((rows, width), BF16),
            pltpu.VMEM((rows, width), BF16),
            pltpu.VMEM((heads * rows, HD), BF16),
            pltpu.VMEM((seqs, 2, rows, HD), BF16),
            pltpu.VMEM((seqs, heads * rows, rows), F32),
            pltpu.VMEM((rows, width), BF16),
            pltpu.VMEM((rows, width), BF16),
            pltpu.VMEM((cols, rows, out_width), F32),
            pltpu.VMEM((cols, rows, out_width), BF16),
            pltpu.VMEM((cols, rows, out_width), BF16),
            pltpu.SemaphoreType.DMA((8,)),
            pltpu.SemaphoreType.DMA((cols, 2)),
            pltpu.SemaphoreType.DMA((3,)),
            pltpu.SemaphoreType.DMA((3,)),
            pltpu.SemaphoreType.DMA((seqs,)),
            pltpu.SemaphoreType.DMA((seqs,)),
            pltpu.SemaphoreType.DMA((cols,)),
            pltpu.SemaphoreType.DMA((cols,)),
        ],
        compiler_params=pltpu.CompilerParams(
            collective_id=0, has_side_effects=True, vmem_limit_bytes=48 * 2**20
        ),
    )(block_order, tokens, query_weight, key_weight, value_weight, output_weight, jnp.asarray(table))


def solution(mesh):
    placed = (
        P("seq", "row"),
        P(),
        P("row", "col"),
        P("row", "col"),
        P("row", "col"),
        P("col", None),
    )
    return jax.shard_map(
        partial(body, mesh.shape["seq"], mesh.shape["col"]),
        mesh=mesh, in_specs=placed, out_specs=P("seq", ("row", "col")), check_vma=False,
    )
```

```python
from functools import partial

import jax
import jax.numpy as jnp
import numpy as np
from jax import lax
from jax.experimental import pallas as pl
from jax.experimental.pallas import tpu as pltpu
from jax.sharding import PartitionSpec as P

H = 32
KV = 8
HD = 128
THETA = 500000.0
HIDDEN = -1e30
WIDE = 256
F32 = jnp.float32
BF16 = jnp.bfloat16


def rotary_table(half_rows, blocks):
    freqs = THETA ** (-2.0 * np.arange(HD // 2) / HD)
    starts = np.concatenate([np.arange(half_rows), half_rows * np.arange(blocks)])
    angles = starts[:, None] * freqs[None, :]
    cosine, sine = np.cos(angles), np.sin(angles)
    return np.concatenate([cosine, cosine, -sine, sine], axis=1).astype(np.float32)


def flip(index, mask):
    for bit in range(mask.bit_length()):
        if mask >> bit & 1:
            index = index + (1 - 2 * (index // 2**bit % 2)) * 2**bit
    return index


def each(first, last, step):
    if last - first <= 8:
        for index in range(first, last):
            step(index)
    else:
        lax.fori_loop(first, last, lambda index, _: (step(index), 0)[1], 0)


def layer_kernel(
    seqs, cols,
    order_ref, x_hbm, wq_hbm, wk_hbm, wv_hbm, wo_hbm, table_hbm,
    out_ref,
    x, wkv, wq, wo, table, rot,
    kv_snd, kv_rcv, q_snd, q_rcv, q, kv, att, att_peer, partial_own, rs_snd, rs_rcv,
    load_sem, wo_sem, core_send, core_recv, seq_send, seq_recv, col_send, col_recv,
):
    rows = x.shape[0]
    half = rows // 2
    heads = wq.shape[1] // 2 // HD
    width = heads * HD
    group = H // KV
    out_width = wo.shape[2]

    me_seq = lax.axis_index("seq")
    me_row = lax.axis_index("row")
    me_col = lax.axis_index("col")
    other = 1 - me_row

    def kv_columns(row):
        return pl.ds(pl.multiple_of(row * heads // group * HD, HD), HD)

    def q_columns(row):
        return pl.ds(pl.multiple_of(row * width, width), width)

    loads = [pltpu.make_async_copy(x_hbm, x, load_sem.at[0])]
    for slot, (source, row) in enumerate(
        [(wk_hbm, other), (wv_hbm, other), (wk_hbm, me_row), (wv_hbm, me_row)]
    ):
        loads.append(
            pltpu.make_async_copy(
                source.at[:, kv_columns(row)],
                wkv.at[:, pl.ds(slot * HD, HD)],
                load_sem.at[1 + slot],
            )
        )
    loads.append(pltpu.make_async_copy(table_hbm, table, load_sem.at[7]))
    for slot, row in enumerate([other, me_row]):
        loads.append(
            pltpu.make_async_copy(
                wq_hbm.at[:, q_columns(row)],
                wq.at[:, pl.ds(slot * width, width)],
                load_sem.at[5 + slot],
            )
        )
    for load in loads:
        load.start()
    load_x, load_kv, load_table, load_q = loads[0], loads[1:5], loads[5], loads[6:]

    def wo_load(step, part):
        target = flip(me_col, step)
        row = me_row if part == 0 else other
        first = pl.multiple_of((me_row * cols + target) * out_width, out_width)
        return pltpu.make_async_copy(
            wo_hbm.at[q_columns(row), pl.ds(first, out_width)],
            wo.at[step, pl.ds(part * width, width), :],
            wo_sem.at[step, part],
        )

    for part in range(2):
        for step in list(range(cols - 1, -1, -1)):
            wo_load(step, part).start()

    barrier = pltpu.get_barrier_semaphore()
    pl.semaphore_signal(barrier, inc=1, device_id={"row": other})
    each(1, seqs, lambda d: pl.semaphore_signal(
        barrier, inc=1, device_id={"seq": lax.rem(me_seq + d, seqs)}))
    each(1, cols, lambda d: pl.semaphore_signal(
        barrier, inc=1, device_id={"col": lax.rem(me_col + d, cols)}))

    load_table.wait()
    for part in range(2):
        cos_in = table[0:half, 0:HD]
        sin_in = table[0:half, HD:]
        start = table[pl.ds(half + order_ref[2 * me_seq + part], 1), :]
        cos_at, sin_at = start[:, :HD], start[:, HD:]
        here = pl.ds(part * half, half)
        rot[0, here, :] = cos_at * cos_in - sin_at * sin_in
        rot[1, here, :] = sin_at * cos_in + cos_at * sin_in

    def rotate(vectors, here):
        return vectors * rot[0, here] + pltpu.roll(vectors, HD // 2, 1) * rot[1, here]

    halves = [slice(0, half), slice(half, rows)]

    def to_core(source, target, index):
        return pltpu.make_async_remote_copy(
            src_ref=source, dst_ref=target,
            send_sem=core_send.at[index], recv_sem=core_recv.at[index],
            device_id={"row": other},
        )

    load_x.wait()
    load_kv[0].wait()
    load_kv[1].wait()
    kv_snd[...] = jnp.dot(x[...], wkv[:, : 2 * HD], preferred_element_type=F32).astype(kv_snd.dtype)
    pl.semaphore_wait(barrier, 1 + (seqs - 1) + (cols - 1))
    send_kv = to_core(kv_snd, kv_rcv, 0)
    send_kv.start()
    load_kv[2].wait()
    load_kv[3].wait()
    kv_own = jnp.dot(x[...], wkv[:, 2 * HD :], preferred_element_type=F32)
    send_kv.wait_recv()

    def seq_copy(part, d, source):
        return pltpu.make_async_remote_copy(
            src_ref=kv.at[source, part], dst_ref=kv.at[source, part],
            send_sem=seq_send.at[part, d], recv_sem=seq_recv.at[part, d],
            device_id={"seq": lax.rem(me_seq + d, seqs)},
        )

    def to_seq(part, d):
        return seq_copy(part, d, me_seq)

    def from_seq(part, d):
        return seq_copy(part, d, lax.rem(me_seq - d + seqs, seqs))

    for part, here in enumerate(halves):
        kv_sum = kv_own[here] + kv_rcv[here, :].astype(F32)
        kv[me_seq, part, 0] = rotate(kv_sum[:, :HD], here).astype(BF16)
        kv[me_seq, part, 1] = kv_sum[:, HD:].astype(BF16)
        each(1, seqs, lambda d: to_seq(part, d).start())

    load_q[0].wait()
    for first in range(0, width, WIDE):
        q_snd[:, first : first + WIDE] = jnp.dot(
            x[...], wq[:, first : first + WIDE], preferred_element_type=F32
        ).astype(q_snd.dtype)
    send_q = to_core(q_snd, q_rcv, 1)
    send_q.start()
    load_q[1].wait()
    own = [
        jnp.dot(x[...], wq[:, width + first : width + first + WIDE], preferred_element_type=F32)
        for first in range(0, width, WIDE)
    ]
    send_q.wait_recv()
    for head in range(heads):
        at = head * HD
        summed = own[at // WIDE][:, at % WIDE : at % WIDE + HD] + q_rcv[:, at : at + HD].astype(F32)
        for part, here in enumerate(halves):
            q[part, head * half : (head + 1) * half, :] = rotate(summed[here], here).astype(BF16)

    stride = 4 if seqs % 4 == 0 else 1
    factor = HD ** -0.5 * float(np.log2(np.e))
    lane = lax.broadcasted_iota(jnp.int32, (1, stride * half), 1)
    row = lax.rem(lax.broadcasted_iota(jnp.int32, (heads * half, 1), 0), half)

    def attend(part, key_part, index, state):
        first = index * stride
        keys = jnp.concatenate([kv[first + i, key_part, 0] for i in range(stride)], axis=0)
        values = jnp.concatenate([kv[first + i, key_part, 1] for i in range(stride)], axis=0)
        scores = lax.dot_general(
            q[part], keys, (((1,), (1,)), ((), ())), preferred_element_type=F32
        )
        if part == key_part:
            key_pos = order_ref[2 * first + part] * half + lane
            for i in range(1, stride):
                start = order_ref[2 * (first + i) + part] * half
                key_pos = jnp.where(lane >= i * half, start + lane - i * half, key_pos)
            visible = key_pos <= order_ref[2 * me_seq + part] * half + row
            scores = jnp.where(visible, scores, HIDDEN)
        top = jnp.max(scores, axis=1, keepdims=True)
        if state is not None:
            top = jnp.maximum(top, state[0])
        weights = jnp.exp2((scores - top) * factor)
        if part == key_part:
            weights = jnp.where(visible, weights, 0.0)
        total = jnp.sum(weights, axis=1, keepdims=True)
        mixed = jnp.dot(weights.astype(BF16), values, preferred_element_type=F32)
        if state is not None:
            rescale = jnp.exp2((state[0] - top) * factor)
            total = total + state[1] * rescale
            mixed = mixed + state[2] * rescale
        return top, total, mixed

    def attend_all(part, key_part, state):
        if seqs == stride:
            return attend(part, key_part, 0, state)
        if state is None:
            state = (
                jnp.full((heads * half, 1), HIDDEN, F32),
                jnp.zeros((heads * half, 1), F32),
                jnp.zeros((heads * half, HD), F32),
            )
        return lax.fori_loop(0, seqs // stride, partial(attend, part, key_part), state)

    def send_attended(part, state):
        attended = (state[2] / state[1]).astype(BF16)
        for head in range(heads):
            att[part, :, head * HD : (head + 1) * HD] = attended[head * half : (head + 1) * half]
        att_copy(part).start()

    def att_copy(part):
        return to_core(att.at[part], att_peer.at[part], 2 + part)

    steps = list(range(cols - 1, -1, -1))

    def to_col(part, d):
        return pltpu.make_async_remote_copy(
            src_ref=rs_snd.at[d, part], dst_ref=rs_rcv.at[d, part],
            send_sem=col_send.at[d, part], recv_sem=col_recv.at[d, part],
            device_id={"col": flip(me_col, d)},
        )

    def own_sums(part):
        for step in steps:
            if part == 0:
                wo_load(step, 0).wait()
            partial_own[step, part] = jnp.dot(
                att[part], wo[step, :width, :], preferred_element_type=F32
            )

    def send_sums(part):
        att_copy(part).wait_recv()
        for step in steps:
            if part == 0:
                wo_load(step, 1).wait()
            summed = partial_own[step, part] + jnp.dot(
                att_peer[part], wo[step, width:, :], preferred_element_type=F32
            )
            if step == 0:
                partial_own[0, part] = summed
            else:
                rs_snd[step, part] = summed.astype(rs_snd.dtype)
                to_col(part, step).start()

    def finish(part):
        final = partial_own[0, part]
        for d in range(1, cols):
            to_col(part, d).wait_recv()
            final = final + rs_rcv[d, part].astype(F32)
        out_ref[halves[part], :] = final

    each(1, seqs, lambda d: from_seq(0, d).wait_recv())
    send_attended(0, attend_all(0, 0, None))
    own_sums(0)
    upper = attend_all(1, 0, None)
    send_sums(0)
    each(1, seqs, lambda d: from_seq(1, d).wait_recv())
    send_attended(1, attend_all(1, 1, upper))
    own_sums(1)
    send_sums(1)
    finish(0)
    finish(1)

    send_kv.wait_send()
    send_q.wait_send()
    for part in range(2):
        att_copy(part).wait_send()
        each(1, seqs, lambda d: to_seq(part, d).wait_send())
        for d in range(1, cols):
            to_col(part, d).wait_send()


def body(seqs, cols, tokens, block_order, query_weight, key_weight, value_weight, output_weight):
    rows, depth = tokens.shape
    width = query_weight.shape[1] // 2
    out_width = output_weight.shape[1] // (2 * cols)
    heads = width // HD
    table = rotary_table(rows // 2, block_order.shape[0])
    anywhere = pl.BlockSpec(memory_space=pl.ANY)
    return pl.pallas_call(
        partial(layer_kernel, seqs, cols),
        out_shape=pltpu.VMEM((rows, out_width), F32),
        in_specs=[pl.BlockSpec(memory_space=pltpu.SMEM)] + [anywhere] * 6,
        out_specs=pl.BlockSpec(memory_space=pltpu.VMEM),
        scratch_shapes=[
            pltpu.VMEM((rows, depth), BF16),
            pltpu.VMEM((depth, 4 * HD), BF16),
            pltpu.VMEM((depth, 2 * width), BF16),
            pltpu.VMEM((cols, 2 * width, out_width), BF16),
            pltpu.VMEM(table.shape, F32),
            pltpu.VMEM((2, rows, HD), F32),
            pltpu.VMEM((rows, 2 * HD), BF16),
            pltpu.VMEM((rows, 2 * HD), BF16),
            pltpu.VMEM((rows, width), BF16),
            pltpu.VMEM((rows, width), BF16),
            pltpu.VMEM((2, heads * rows // 2, HD), BF16),
            pltpu.VMEM((seqs, 2, 2, rows // 2, HD), BF16),
            pltpu.VMEM((2, rows // 2, width), BF16),
            pltpu.VMEM((2, rows // 2, width), BF16),
            pltpu.VMEM((cols, 2, rows // 2, out_width), F32),
            pltpu.VMEM((cols, 2, rows // 2, out_width), BF16),
            pltpu.VMEM((cols, 2, rows // 2, out_width), BF16),
            pltpu.SemaphoreType.DMA((8,)),
            pltpu.SemaphoreType.DMA((cols, 2)),
            pltpu.SemaphoreType.DMA((4,)),
            pltpu.SemaphoreType.DMA((4,)),
            pltpu.SemaphoreType.DMA((2, seqs)),
            pltpu.SemaphoreType.DMA((2, seqs)),
            pltpu.SemaphoreType.DMA((cols, 2)),
            pltpu.SemaphoreType.DMA((cols, 2)),
        ],
        compiler_params=pltpu.CompilerParams(
            collective_id=0, has_side_effects=True, vmem_limit_bytes=60 * 2**20
        ),
    )(block_order, tokens, query_weight, key_weight, value_weight, output_weight, jnp.asarray(table))


def solution(mesh):
    placed = (
        P("seq", "row"),
        P(),
        P("row", "col"),
        P("row", "col"),
        P("row", "col"),
        P("col", None),
    )
    return jax.shard_map(
        partial(body, mesh.shape["seq"], mesh.shape["col"]),
        mesh=mesh, in_specs=placed, out_specs=P("seq", ("row", "col")), check_vma=False,
    )
```

```python
from functools import partial

import jax
import jax.numpy as jnp
import numpy as np
from jax import lax
from jax.experimental import pallas as pl
from jax.experimental.pallas import tpu as pltpu
from jax.sharding import PartitionSpec as P

H = 32
KV = 8
HD = 128
THETA = 500000.0
HIDDEN = -1e30
WIDE = 256
F32 = jnp.float32
BF16 = jnp.bfloat16


def rotary_table(half_rows, blocks):
    freqs = THETA ** (-2.0 * np.arange(HD // 2) / HD)
    starts = np.concatenate([np.arange(half_rows), half_rows * np.arange(blocks)])
    angles = starts[:, None] * freqs[None, :]
    cosine, sine = np.cos(angles), np.sin(angles)
    return np.concatenate([cosine, cosine, -sine, sine], axis=1).astype(np.float32)


def flip(index, mask):
    for bit in range(mask.bit_length()):
        if mask >> bit & 1:
            index = index + (1 - 2 * (index // 2**bit % 2)) * 2**bit
    return index


def each(first, last, step):
    if last - first <= 8:
        for index in range(first, last):
            step(index)
    else:
        lax.fori_loop(first, last, lambda index, _: (step(index), 0)[1], 0)


def layer_kernel(
    seqs, cols,
    order_hbm, x_hbm, wq_hbm, wk_hbm, wv_hbm, wo_hbm, table_hbm,
    out_ref,
    x, wkv, wq, wo, table, rot,
    kv_snd, kv_rcv, q_snd, q_rcv, q, kv, att, att_peer, partial_own, rs_snd, rs_rcv,
    order_ref, load_sem, wo_sem, core_send, core_recv, seq_send, seq_recv, col_send, col_recv,
):
    rows = x.shape[0]
    half = rows // 2
    heads = wq.shape[1] // 2 // HD
    width = heads * HD
    group = H // KV
    out_width = wo.shape[2]

    me_seq = lax.axis_index("seq")
    me_row = lax.axis_index("row")
    me_col = lax.axis_index("col")
    other = 1 - me_row

    def kv_columns(row):
        return pl.ds(pl.multiple_of(row * heads // group * HD, HD), HD)

    def q_columns(row):
        return pl.ds(pl.multiple_of(row * width, width), width)

    barrier = pltpu.get_barrier_semaphore()
    pl.semaphore_signal(barrier, inc=1, device_id={"row": other})
    each(1, seqs, lambda d: pl.semaphore_signal(
        barrier, inc=1, device_id={"seq": lax.rem(me_seq + d, seqs)}))
    each(1, cols, lambda d: pl.semaphore_signal(
        barrier, inc=1, device_id={"col": lax.rem(me_col + d, cols)}))

    loads = [pltpu.make_async_copy(x_hbm, x, load_sem.at[0])]
    for slot, (source, row) in enumerate(
        [(wk_hbm, other), (wv_hbm, other), (wk_hbm, me_row), (wv_hbm, me_row)]
    ):
        loads.append(
            pltpu.make_async_copy(
                source.at[:, kv_columns(row)],
                wkv.at[:, pl.ds(slot * HD, HD)],
                load_sem.at[1 + slot],
            )
        )
    loads.append(pltpu.make_async_copy(table_hbm, table, load_sem.at[7]))
    for slot, row in enumerate([other, me_row]):
        loads.append(
            pltpu.make_async_copy(
                wq_hbm.at[:, q_columns(row)],
                wq.at[:, pl.ds(slot * width, width)],
                load_sem.at[5 + slot],
            )
        )
    for load in loads:
        load.start()
    load_order = pltpu.make_async_copy(order_hbm, order_ref, load_sem.at[8])
    load_order.start()
    load_x, load_kv, load_table, load_q = loads[0], loads[1:5], loads[5], loads[6:]

    def wo_load(step, part):
        target = flip(me_col, step)
        row = me_row if part == 0 else other
        first = pl.multiple_of((me_row * cols + target) * out_width, out_width)
        return pltpu.make_async_copy(
            wo_hbm.at[q_columns(row), pl.ds(first, out_width)],
            wo.at[step, pl.ds(part * width, width), :],
            wo_sem.at[step, part],
        )

    for part in range(2):
        for step in list(range(cols - 1, -1, -1)):
            wo_load(step, part).start()

    load_table.wait()
    load_order.wait()
    for part in range(2):
        cos_in = table[0:half, 0:HD]
        sin_in = table[0:half, HD:]
        start = table[pl.ds(half + order_ref[2 * me_seq + part], 1), :]
        cos_at, sin_at = start[:, :HD], start[:, HD:]
        here = pl.ds(part * half, half)
        rot[0, here, :] = cos_at * cos_in - sin_at * sin_in
        rot[1, here, :] = sin_at * cos_in + cos_at * sin_in

    def rotate(vectors, here):
        return vectors * rot[0, here] + pltpu.roll(vectors, HD // 2, 1) * rot[1, here]

    halves = [slice(0, half), slice(half, rows)]

    def to_core(source, target, index):
        return pltpu.make_async_remote_copy(
            src_ref=source, dst_ref=target,
            send_sem=core_send.at[index], recv_sem=core_recv.at[index],
            device_id={"row": other},
        )

    load_x.wait()
    load_kv[0].wait()
    load_kv[1].wait()
    kv_snd[...] = jnp.dot(x[...], wkv[:, : 2 * HD], preferred_element_type=F32).astype(kv_snd.dtype)
    pl.semaphore_wait(barrier, 1 + (seqs - 1) + (cols - 1))
    send_kv = to_core(kv_snd, kv_rcv, 0)
    send_kv.start()
    load_kv[2].wait()
    load_kv[3].wait()
    kv_own = jnp.dot(x[...], wkv[:, 2 * HD :], preferred_element_type=F32)
    send_kv.wait_recv()

    def seq_copy(part, d, source):
        return pltpu.make_async_remote_copy(
            src_ref=kv.at[source, part], dst_ref=kv.at[source, part],
            send_sem=seq_send.at[part, d], recv_sem=seq_recv.at[part, d],
            device_id={"seq": lax.rem(me_seq + d, seqs)},
        )

    def to_seq(part, d):
        return seq_copy(part, d, me_seq)

    def from_seq(part, d):
        return seq_copy(part, d, lax.rem(me_seq - d + seqs, seqs))

    for part, here in enumerate(halves):
        kv_sum = kv_own[here] + kv_rcv[here, :].astype(F32)
        kv[me_seq, part, 0] = rotate(kv_sum[:, :HD], here).astype(BF16)
        kv[me_seq, part, 1] = kv_sum[:, HD:].astype(BF16)
        each(1, seqs, lambda d: to_seq(part, d).start())

    load_q[0].wait()
    for first in range(0, width, WIDE):
        q_snd[:, first : first + WIDE] = jnp.dot(
            x[...], wq[:, first : first + WIDE], preferred_element_type=F32
        ).astype(q_snd.dtype)
    send_q = to_core(q_snd, q_rcv, 1)
    send_q.start()
    load_q[1].wait()
    own = [
        jnp.dot(x[...], wq[:, width + first : width + first + WIDE], preferred_element_type=F32)
        for first in range(0, width, WIDE)
    ]
    send_q.wait_recv()
    for head in range(heads):
        at = head * HD
        summed = own[at // WIDE][:, at % WIDE : at % WIDE + HD] + q_rcv[:, at : at + HD].astype(F32)
        for part, here in enumerate(halves):
            q[part, head * half : (head + 1) * half, :] = rotate(summed[here], here).astype(BF16)

    stride = 4 if seqs % 4 == 0 else 1
    factor = HD ** -0.5 * float(np.log2(np.e))
    lane = lax.broadcasted_iota(jnp.int32, (1, stride * half), 1)
    row = lax.rem(lax.broadcasted_iota(jnp.int32, (heads * half, 1), 0), half)

    def attend(part, key_part, index, state):
        first = index * stride
        keys = jnp.concatenate([kv[first + i, key_part, 0] for i in range(stride)], axis=0)
        values = jnp.concatenate([kv[first + i, key_part, 1] for i in range(stride)], axis=0)
        scores = lax.dot_general(
            q[part], keys, (((1,), (1,)), ((), ())), preferred_element_type=F32
        )
        if part == key_part:
            key_pos = order_ref[2 * first + part] * half + lane
            for i in range(1, stride):
                start = order_ref[2 * (first + i) + part] * half
                key_pos = jnp.where(lane >= i * half, start + lane - i * half, key_pos)
            visible = key_pos <= order_ref[2 * me_seq + part] * half + row
            scores = jnp.where(visible, scores, HIDDEN)
        top = jnp.max(scores, axis=1, keepdims=True)
        if state is not None:
            top = jnp.maximum(top, state[0])
        weights = jnp.exp2((scores - top) * factor)
        if part == key_part:
            weights = jnp.where(visible, weights, 0.0)
        total = jnp.sum(weights, axis=1, keepdims=True)
        mixed = jnp.dot(weights.astype(BF16), values, preferred_element_type=F32)
        if state is not None:
            rescale = jnp.exp2((state[0] - top) * factor)
            total = total + state[1] * rescale
            mixed = mixed + state[2] * rescale
        return top, total, mixed

    def attend_all(part, key_part, state):
        if seqs == stride:
            return attend(part, key_part, 0, state)
        if state is None:
            state = (
                jnp.full((heads * half, 1), HIDDEN, F32),
                jnp.zeros((heads * half, 1), F32),
                jnp.zeros((heads * half, HD), F32),
            )
        return lax.fori_loop(0, seqs // stride, partial(attend, part, key_part), state)

    def send_attended(part, state):
        attended = (state[2] / state[1]).astype(BF16)
        for head in range(heads):
            att[part, :, head * HD : (head + 1) * HD] = attended[head * half : (head + 1) * half]
        att_copy(part).start()

    def att_copy(part):
        return to_core(att.at[part], att_peer.at[part], 2 + part)

    steps = list(range(cols - 1, -1, -1))

    def to_col(part, d):
        return pltpu.make_async_remote_copy(
            src_ref=rs_snd.at[d, part], dst_ref=rs_rcv.at[d, part],
            send_sem=col_send.at[d, part], recv_sem=col_recv.at[d, part],
            device_id={"col": flip(me_col, d)},
        )

    def own_sums(part):
        for step in steps:
            if part == 0:
                wo_load(step, 0).wait()
            partial_own[step, part] = jnp.dot(
                att[part], wo[step, :width, :], preferred_element_type=F32
            )

    def send_sums(part):
        att_copy(part).wait_recv()
        for step in steps:
            if part == 0:
                wo_load(step, 1).wait()
            summed = partial_own[step, part] + jnp.dot(
                att_peer[part], wo[step, width:, :], preferred_element_type=F32
            )
            if step == 0:
                partial_own[0, part] = summed
            else:
                rs_snd[step, part] = summed.astype(rs_snd.dtype)
                to_col(part, step).start()

    def finish(part):
        final = partial_own[0, part]
        for d in range(1, cols):
            to_col(part, d).wait_recv()
            final = final + rs_rcv[d, part].astype(F32)
        out_ref[halves[part], :] = final

    each(1, seqs, lambda d: from_seq(0, d).wait_recv())
    send_attended(0, attend_all(0, 0, None))
    own_sums(0)
    upper = attend_all(1, 0, None)
    send_sums(0)
    each(1, seqs, lambda d: from_seq(1, d).wait_recv())
    send_attended(1, attend_all(1, 1, upper))
    own_sums(1)
    send_sums(1)
    finish(0)
    finish(1)

    send_kv.wait_send()
    send_q.wait_send()
    for part in range(2):
        att_copy(part).wait_send()
        each(1, seqs, lambda d: to_seq(part, d).wait_send())
        for d in range(1, cols):
            to_col(part, d).wait_send()


def body(seqs, cols, tokens, block_order, query_weight, key_weight, value_weight, output_weight):
    rows, depth = tokens.shape
    width = query_weight.shape[1] // 2
    out_width = output_weight.shape[1] // (2 * cols)
    heads = width // HD
    table = rotary_table(rows // 2, block_order.shape[0])
    anywhere = pl.BlockSpec(memory_space=pl.ANY)
    return pl.pallas_call(
        partial(layer_kernel, seqs, cols),
        out_shape=pltpu.VMEM((rows, out_width), F32),
        in_specs=[anywhere] * 7,
        out_specs=pl.BlockSpec(memory_space=pltpu.VMEM),
        scratch_shapes=[
            pltpu.VMEM((rows, depth), BF16),
            pltpu.VMEM((depth, 4 * HD), BF16),
            pltpu.VMEM((depth, 2 * width), BF16),
            pltpu.VMEM((cols, 2 * width, out_width), BF16),
            pltpu.VMEM(table.shape, F32),
            pltpu.VMEM((2, rows, HD), F32),
            pltpu.VMEM((rows, 2 * HD), BF16),
            pltpu.VMEM((rows, 2 * HD), BF16),
            pltpu.VMEM((rows, width), BF16),
            pltpu.VMEM((rows, width), BF16),
            pltpu.VMEM((2, heads * rows // 2, HD), BF16),
            pltpu.VMEM((seqs, 2, 2, rows // 2, HD), BF16),
            pltpu.VMEM((2, rows // 2, width), BF16),
            pltpu.VMEM((2, rows // 2, width), BF16),
            pltpu.VMEM((cols, 2, rows // 2, out_width), F32),
            pltpu.VMEM((cols, 2, rows // 2, out_width), BF16),
            pltpu.VMEM((cols, 2, rows // 2, out_width), BF16),
            pltpu.SMEM(block_order.shape, jnp.int32),
            pltpu.SemaphoreType.DMA((9,)),
            pltpu.SemaphoreType.DMA((cols, 2)),
            pltpu.SemaphoreType.DMA((4,)),
            pltpu.SemaphoreType.DMA((4,)),
            pltpu.SemaphoreType.DMA((2, seqs)),
            pltpu.SemaphoreType.DMA((2, seqs)),
            pltpu.SemaphoreType.DMA((cols, 2)),
            pltpu.SemaphoreType.DMA((cols, 2)),
        ],
        compiler_params=pltpu.CompilerParams(
            collective_id=0, has_side_effects=True, vmem_limit_bytes=60 * 2**20
        ),
    )(block_order, tokens, query_weight, key_weight, value_weight, output_weight, jnp.asarray(table))


def solution(mesh):
    placed = (
        P("seq", "row"),
        P(),
        P("row", "col"),
        P("row", "col"),
        P("row", "col"),
        P("col", None),
    )
    return jax.shard_map(
        partial(body, mesh.shape["seq"], mesh.shape["col"]),
        mesh=mesh, in_specs=placed, out_specs=P("seq", ("row", "col")), check_vma=False,
    )
```
